32 devices in a mesh: tm: 4 (over y, x), azim: 8 (over z, core).
Axes of the slice: x: 2, y: 2, z: 4, core: 2. Of those that a mesh axis runs over, the one named last changes fastest.
Arguments:
- rotor_coeffs: float32 [64, 2, 8, 16384], P('tm', None, 'azim'), may hold values from -1.5 to 1.5
- mortar_weights: float32 [64, 2, 8, 16384], P('tm', None, 'azim'), may hold values from 0.2 to 1
- block_shifts: int32 [64], P('tm'), may hold values from 0 to 7
- stencil_offsets: int32 [64, 2], P('tm'), may hold values from -1 to 1
- reluctivity: float32 [8, 16384], P('azim'), may hold values from 0.5 to 2
- source: float32 [64, 2, 8, 16384], P('tm', None, 'azim'), may hold values from -3 to 3
Outputs:
- residual: float32 [64, 2, 8, 16384], P('tm', None, 'azim')
The draws below stay inside these ranges and needn't reach their ends.
All inputs are finite; a program needn't handle non-finite values.
Results may differ from the reference program's by a relative error of at most 0.0001.
Values sent between devices are 32-bit elements; how exact they have to be, the bound alone decides.
No kernel may reach another device: no remote copies, remote signals or barrier semaphores. Data moves between devices by JAX's collectives and lax.ppermute only.
A program may use at most 128 MiB of HBM per device.

```python
import math
import jax
import jax.numpy as jnp
from jax import lax

KC = 64
NT = 64
COMP = 2
STEN = 2
P_SIZE = 16384
NB = 8


def set_ends(entries, rng, low, top_value):
    place = [jax.random.randint(jax.random.fold_in(rng, axis), (), 0, length) for axis, length in enumerate(entries.shape)]
    main_axis = entries.shape.index(max(entries.shape))
    next_to = place[:main_axis] + [(place[main_axis] + 1) % entries.shape[main_axis]] + place[main_axis + 1:]
    return entries.at[tuple(place)].set(low).at[tuple(next_to)].set(top_value)


def levels(stream_key, dims, split, low, top_value):
    loudness = 1.0
    for dim, parts in split:
        draws = jax.random.uniform(jax.random.fold_in(jax.random.fold_in(stream_key, 6), dim), (parts,), jnp.float32, low / len(split), top_value / len(split))
        loudness = loudness * jnp.repeat(jnp.exp(draws), dims[dim] // parts).reshape((-1,) + (1,) * (len(dims) - 1 - dim))
    return loudness


def centred(rng, shape, scale, reach, pieces=(), kind=jnp.bfloat16):
    gain = levels(rng, shape, pieces, -0.22, 0.18) if pieces else 1.0
    array = jax.random.normal(rng, shape, jnp.float32) * scale * gain
    return jnp.minimum(jnp.maximum(array, -reach), reach).astype(kind)


def setup_inputs(seed: int = 0) -> dict:
    seeds = jax.random.split(jax.random.key(seed), 7)
    return {
        "rotor_coeffs": centred(seeds[0], (KC, COMP, NB, P_SIZE), 0.25, 1.5, ((0, 4), (2, 8)), jnp.float32),
        "mortar_weights": jnp.clip(0.2 + 0.8 * jax.random.uniform(seeds[1], (NT, STEN, NB, P_SIZE), jnp.float32) ** levels(seeds[1], (NT, STEN, NB, P_SIZE), ((0, 4), (2, 8)), -0.2, 0.2), 0.2, 1.0),
        "block_shifts": set_ends(jax.random.randint(seeds[2], (NT,), 0, NB), jax.random.fold_in(seeds[2], 1), 0, NB - 1).astype(jnp.int32),
        "stencil_offsets": set_ends(jax.random.randint(seeds[3], (NT, STEN), -1, 2), jax.random.fold_in(seeds[3], 1), -1, 1).astype(jnp.int32),
        "reluctivity": jnp.clip(jnp.exp(math.log(2.0) - 1.3862944 * jax.random.uniform(seeds[4], (NB, P_SIZE), jnp.float32) ** levels(seeds[4], (NB, P_SIZE), ((0, 8),), -0.2, 0.2)), 0.5, 2.0),
        "source": centred(seeds[5], (KC, COMP, NB, P_SIZE), 0.5, 3.0, ((0, 4), (2, 8)), jnp.float32),
    }


def harmonic_basis(sample_rows, coefficient_count):
    column = jnp.arange(coefficient_count, dtype=jnp.int32)
    harmonic_order = 2 * (column // 2) + 1
    phase_index = (harmonic_order[None, :] * (2 * sample_rows[:, None] + 1)) % (4 * NT)
    phase_angle = phase_index.astype(jnp.float32) * (jnp.pi / (2 * NT))
    return jnp.where(column[None, :] % 2 == 0, jnp.cos(phase_angle), jnp.sin(phase_angle))


def reference(rotor_coeffs, mortar_weights, block_shifts, stencil_offsets, reluctivity, source):
    basis_table = harmonic_basis(jnp.arange(NT, dtype=jnp.int32), KC)
    forward_scale = 2.0 / NT

    def one_sample(accumulated, inputs):
        basis_row, weights, shift_amount, offsets = inputs
        sample = jnp.tensordot(basis_row, rotor_coeffs, axes=(0, 0), precision=lax.Precision.HIGHEST)
        turned = jnp.roll(sample, shift_amount, axis=1)
        airgap_field = jnp.zeros_like(sample)
        for stencil_entry in range(STEN):
            airgap_field = airgap_field + weights[stencil_entry][None] * jnp.roll(turned, -offsets[stencil_entry], axis=1)
        square = jnp.sum(airgap_field * airgap_field, axis=0)
        field_flux = (reluctivity * (1.0 + square / (1.0 + square)))[None] * airgap_field
        accumulated = accumulated + forward_scale * basis_row[:, None, None, None] * field_flux[None]
        return accumulated, None

    start_value = jnp.zeros((KC, COMP, NB, P_SIZE), jnp.float32)
    accumulated, unused = lax.scan(one_sample, start_value, (basis_table, mortar_weights, block_shifts, stencil_offsets))
    return accumulated - source
```

```python
import functools

import jax
import jax.numpy as jnp
import ml_dtypes
import numpy as np
from jax import lax
from jax.experimental import pallas as pl
from jax.experimental.pallas import tpu as pltpu
from jax.sharding import PartitionSpec as P

LANES = 128
CHUNKS = 4
VMEM = pl.BlockSpec(memory_space=pltpu.VMEM)
SMEM = pl.BlockSpec(memory_space=pltpu.SMEM)
LIMIT = 48 * 1024 * 1024


def basis_table(sample_count, coefficient_count):
    column = np.arange(coefficient_count)
    order = 2 * (column // 2) + 1
    phase = order[None, :] * (2 * np.arange(sample_count)[:, None] + 1) % (4 * sample_count)
    angle = phase * (np.pi / (2 * sample_count))
    return np.where(column[None, :] % 2 == 0, np.cos(angle), np.sin(angle)).astype(np.float32)


def split_table(table):
    high = table.astype(ml_dtypes.bfloat16)
    low = (table - high.astype(np.float32)).astype(ml_dtypes.bfloat16)
    return np.concatenate([high, high, low], axis=1)


def table_dot(parts, value):
    high = value.astype(jnp.bfloat16)
    low = (value - high.astype(jnp.float32)).astype(jnp.bfloat16)
    return jnp.dot(
        parts, jnp.concatenate([high, low, high], axis=0), preferred_element_type=jnp.float32
    )


def call(kernel, out_shape, inputs, scratch=(), flops=0):
    size = sum(4 * np.prod(x.shape) for x in (*inputs, *out_shape))
    return pl.pallas_call(
        kernel,
        out_shape=[jax.ShapeDtypeStruct(x.shape, x.dtype) for x in out_shape],
        in_specs=[SMEM] + [VMEM] * (len(inputs) - 1),
        out_specs=[VMEM] * len(out_shape),
        scratch_shapes=list(scratch),
        compiler_params=pltpu.CompilerParams(vmem_limit_bytes=LIMIT),
        cost_estimate=pl.CostEstimate(flops=flops, bytes_accessed=int(size), transcendentals=0),
    )(*inputs)


def f32(*shape):
    return jax.ShapeDtypeStruct(shape, jnp.float32)


def xor_permute(value, axis, step):
    count = lax.axis_size(axis)
    return lax.ppermute(value, axis, [(i, i ^ step) for i in range(count)])


def pack_kernel(parts, widths, quarter_rows, place, x, *outs):
    outer = outs[0].shape[1]
    stride = x.shape[0] // outer
    for i in range(parts):
        first = (place[0] ^ i) * quarter_rows
        for comp in range(2):
            r = 0
            for g, width in enumerate(widths):
                for lane in range(0, width, LANES):
                    start = comp * (stride // 2) + first + r
                    outs[i * len(widths) + g][comp, :, lane : lane + LANES] = x[
                        pl.ds(start, outer, stride=stride), :
                    ]
                    r += 1


def gather_kernel(parts, chunk_count, place, *refs):
    pieces, outs = refs[:parts], refs[parts:]
    rows = pieces[0].shape[1]
    width = outs[0].shape[2]
    for i in range(parts):
        first = pl.multiple_of((place[0] ^ i) * rows, rows)
        for k in range(chunk_count):
            outs[k][:, pl.ds(first, rows), :] = pieces[i][:, :, k * width : (k + 1) * width]


def in_first(me, base, size, shifts):
    offset = (me - base + 1 + shifts) & (2 * size - 1)
    return ((base - 1 - shifts + offset - me) & (4 * size - 1)) == 0


def choose(me, size, shifts):
    clear = ~(size - 1)
    kept = in_first(me, me & clear, size, shifts)
    sent = in_first(me, (me ^ size) & clear, size, shifts)
    return kept, sent


def is_outer(me, count):
    return ((me // (count // 2)) ^ (me // (count // 4))) & 1 == 0


def sample_step(count, place, table, shifts, own, far, send, keep):
    me = place[1]
    kept, sent = choose(me, count // 4, shifts[0])
    parts = table[...]
    for comp in range(2):
        near_samples = table_dot(parts, own[comp])
        far_samples = table_dot(parts, far[comp])
        for lane in range(0, own.shape[2], LANES):
            here = slice(lane, lane + LANES)
            keep[comp, :, here] = jnp.where(kept, near_samples[:, here], far_samples[:, here])
            send[comp, :, here] = jnp.where(sent, near_samples[:, here], far_samples[:, here])


def first_kernel(count, place, table, shifts, own, arrived, following, send, keep):
    outer = is_outer(place[1], count)

    @pl.when(outer)
    def _():
        send[...] = following[...]
        keep[...] = own[...]

    @pl.when(jnp.logical_not(outer))
    def _():
        sample_step(count, place, table, shifts, own, arrived, send, keep)


def second_kernel(count, place, table, shifts, own, arrived, following, kept, send, keep):
    outer = is_outer(place[1], count)

    @pl.when(outer)
    def _():
        sample_step(count, place, table, shifts, own, arrived, send, keep)

    @pl.when(jnp.logical_not(outer))
    def _():
        send[...] = following[...]
        keep[...] = kept[...]


def middle_kernel(count, size, place, shifts, first, slot_a, slot_b, send, keep):
    me = place[1]
    outer = is_outer(me, count)
    kept, sent = choose(me, size, shifts[0])
    for comp in range(2):
        for lane in range(0, first.shape[2], LANES):
            here = slice(lane, lane + LANES)
            one = first[comp, :, here]
            two = jnp.where(outer, slot_a[comp, :, here], slot_b[comp, :, here])
            keep[comp, :, here] = jnp.where(kept, one, two)
            send[comp, :, here] = jnp.where(sent, one, two)


def flux_kernel(count, parts, row0, lane0, place, table, plan, iron, *refs):
    keep, slot_a, slot_b, far_keep, far_a, far_b = refs[:6]
    weights = refs[6 : 6 + parts]
    outs = refs[6 + parts : 6 + 2 * parts]
    flux, result, ordered = refs[6 + 2 * parts :]
    width = keep.shape[2]
    samples = keep.shape[1]
    rows = samples // parts
    tm, me = place[0], place[1]
    for i in range(parts):
        first = pl.multiple_of((tm ^ i) * rows, rows)
        ordered[:, pl.ds(first, rows), :] = weights[i][:, :, lane0 : lane0 + width]
    source = [((me + plan[1 + m] - plan[0]) ^ me) & 3 for m in range(2)]
    is_near = [s == 0 for s in source]
    is_two = [s == 2 for s in source]
    is_one = [s == 1 for s in source]
    quarter = tm * (iron.shape[0] // parts) + row0

    def fields(slot, far_slot):
        for lane in range(0, width, LANES):
            here = slice(lane, lane + LANES)
            weight = [ordered[m, :, here] for m in range(2)]
            field = []
            for comp in range(2):
                blocks = [ref[comp, :, here] for ref in (keep, slot, far_keep, far_slot)]
                terms = [
                    weight[m]
                    * jnp.where(
                        is_near[m],
                        blocks[0],
                        jnp.where(is_two[m], blocks[1], jnp.where(is_one[m], blocks[2], blocks[3])),
                    )
                    for m in range(2)
                ]
                field.append(terms[0] + terms[1])
            square = field[0] * field[0] + field[1] * field[1]
            gain = iron[pl.ds(quarter + lane // LANES, 1), :] * (1.0 + square / (1.0 + square))
            for comp in range(2):
                flux[:, comp * width + lane : comp * width + lane + LANES] = gain * field[comp]

    outer = is_outer(me, count)

    @pl.when(outer)
    def _():
        fields(slot_a, far_a)

    @pl.when(jnp.logical_not(outer))
    def _():
        fields(slot_b, far_b)

    result[...] = table_dot(table[...], flux[...])
    rows = result.shape[0] // parts
    for i in range(parts):
        first = pl.multiple_of((tm ^ i) * rows, rows)
        for comp in range(2):
            outs[i][comp] = result[pl.ds(first, rows), comp * width : (comp + 1) * width]


def finish_kernel(parts, chunks, quarter_rows, place, source, *refs):
    pieces, out = refs[:-1], refs[-1]
    outer, width = pieces[0].shape[1:]
    stride = source.shape[0] // outer
    for k in range(chunks):
        for i in range(parts):
            piece = pieces[k * parts + i]
            first = (place[0] ^ i) * quarter_rows + k * (width // LANES)
            for comp in range(2):
                for r in range(width // LANES):
                    here = pl.ds(comp * (stride // 2) + first + r, outer, stride=stride)
                    out[here, :] = piece[comp, :, r * LANES : (r + 1) * LANES] - source[here, :]


def body(rotor_coeffs, mortar_weights, block_shifts, stencil_offsets, reluctivity, source):
    parts, count = lax.axis_size("tm"), lax.axis_size("azim")
    coeff_rows, comps, _, nodes = rotor_coeffs.shape
    sample_rows = mortar_weights.shape[0]
    coeffs, samples = coeff_rows * parts, sample_rows * parts
    share = nodes // parts
    chunks = CHUNKS
    width = share // chunks
    share_rows = share // LANES
    place = jnp.stack([lax.axis_index("tm"), lax.axis_index("azim")]).astype(jnp.int32)
    table = basis_table(samples, coeffs)
    forward = jnp.asarray(split_table(table))
    backward = jnp.asarray(split_table(np.ascontiguousarray(table.T) * np.float32(2.0 / samples)))

    def as_rows(x):
        return x.reshape(-1, LANES)

    def pack(x, widths):
        outs = call(
            functools.partial(pack_kernel, parts, widths, share_rows),
            [f32(2, x.shape[0], w) for i in range(parts) for w in widths],
            (place, as_rows(x)),
        )
        return [outs[i * len(widths) : (i + 1) * len(widths)] for i in range(parts)]

    def swap(pieces):
        return [pieces[0]] + [xor_permute(pieces[i], "tm", i) for i in range(1, parts)]

    local_plan = jnp.concatenate([block_shifts[:, None], stencil_offsets], axis=1)
    plan = lax.all_gather(local_plan, "tm", axis=0, tiled=True)
    plan = jnp.broadcast_to(plan.T[:, :, None], (3, samples, LANES))

    packed = pack(rotor_coeffs, (width, share - width))
    head = swap([p[0] for p in packed])
    rest = swap([p[1] for p in packed])

    def gather(pieces, number):
        return call(
            functools.partial(gather_kernel, parts, number),
            [f32(2, coeffs, width)] * number,
            (place, *pieces),
        )

    own = gather(head, 1) + gather(rest, chunks - 1)
    mortar_weights, _ = lax.optimization_barrier((mortar_weights, rest[1]))
    weights = swap([p[0] for p in pack(mortar_weights, (share,))])

    half, fourth = count // 2, count // 4
    outer = [d for d in range(count) if is_outer(d, count)]
    inner = [d for d in range(count) if not is_outer(d, count)]
    coeff_a = [(d, d ^ half) for d in outer]
    coeff_b = [(d, d ^ half) for d in inner]
    sample_a = [(d, d ^ fourth) for d in inner]
    sample_b = [(d, d ^ fourth) for d in outer]
    block = f32(2, samples, width)
    dot_flops = 4 * 2 * samples * 3 * coeffs * width
    slots_a, slots_b, keeps = [], [], []
    send_a = send_b = own[0]
    for k in range(chunks):
        slots_a.append(lax.ppermute(send_a, "azim", coeff_a + (sample_a if k else [])))
        slots_b.append(lax.ppermute(send_b, "azim", coeff_b + (sample_b if k else [])))
        following = own[min(k + 1, chunks - 1)]
        send_a, kept = call(
            functools.partial(first_kernel, count),
            [block, block],
            (place, forward, plan, own[k], slots_a[k], following),
            flops=dot_flops,
        )
        send_b, kept = call(
            functools.partial(second_kernel, count),
            [block, block],
            (place, forward, plan, own[k], slots_b[k], following, kept),
            flops=dot_flops,
        )
        keeps.append(kept)
    slots_a.append(lax.ppermute(send_a, "azim", sample_a))
    slots_b.append(lax.ppermute(send_b, "azim", sample_b))

    pieces = []
    for k in range(chunks):
        keep, slot_a, slot_b = keeps[k], slots_a[k + 1], slots_b[k + 1]
        size = count // 8
        while size >= 2:
            send, keep = call(
                functools.partial(middle_kernel, count, size),
                [block, block],
                (place, plan, keep, slot_a, slot_b),
            )
            slot_a = slot_b = xor_permute(send, "azim", size)
            size //= 2
        far_keep = xor_permute(keep, "azim", 1)
        far_a = xor_permute(slot_a, "azim", 1)
        far_b = far_a if slot_b is slot_a else xor_permute(slot_b, "azim", 1)
        made = call(
            functools.partial(flux_kernel, count, parts, k * (width // LANES), k * width),
            [f32(2, coeff_rows, width)] * parts,
            (
                place,
                backward,
                plan,
                as_rows(reluctivity),
                keep,
                slot_a,
                slot_b,
                far_keep,
                far_a,
                far_b,
                *weights,
            ),
            scratch=(
                pltpu.VMEM((samples, 2 * width), jnp.float32),
                pltpu.VMEM((coeffs, 2 * width), jnp.float32),
                pltpu.VMEM((2, samples, width), jnp.float32),
            ),
            flops=dot_flops // 2,
        )
        pieces += swap(made)
    (out,) = call(
        functools.partial(finish_kernel, parts, chunks, share_rows),
        [f32(coeff_rows * comps * (nodes // LANES), LANES)],
        (place, as_rows(source), *pieces),
    )
    return out.reshape(source.shape)


def solution(mesh):
    wide = P("tm", None, "azim", None)
    in_specs = (wide, wide, P("tm"), P("tm", None), P("azim", None), wide)
    return jax.shard_map(body, mesh=mesh, in_specs=in_specs, out_specs=wide, check_vma=False)
```

```python
import functools

import jax
import jax.numpy as jnp
import ml_dtypes
import numpy as np
from jax import lax
from jax.experimental import pallas as pl
from jax.experimental.pallas import tpu as pltpu
from jax.sharding import PartitionSpec as P

LANES = 128
CHUNK_SHARES = (8, 8, 8, 8)
FLUX_GROUPS = ((0, 1), (2,), (3,))
WEIGHTS_TOGETHER = False
RESULTS_TOGETHER = False
REST_TOGETHER = False
RELEASE = 2
PAIR_AFTER = True
PAIR_GATE = 1
FLUX_GATE = 2
SEEN_GATE = 9
PACK_GATE = 1
WEIGHT_GATE = 3
REST_FIRST = True
HEAD_LIMIT = True
VMEM = pl.BlockSpec(memory_space=pltpu.VMEM)
SMEM = pl.BlockSpec(memory_space=pltpu.SMEM)
HBM = pl.BlockSpec(memory_space=pltpu.HBM)
SUBLANES = 8
LIMIT = 48 * 1024 * 1024
FULL = 62 * 1024 * 1024


def basis_table(sample_count, coefficient_count):
    column = np.arange(coefficient_count)
    order = 2 * (column // 2) + 1
    phase = order[None, :] * (2 * np.arange(sample_count)[:, None] + 1) % (4 * sample_count)
    angle = phase * (np.pi / (2 * sample_count))
    return np.where(column[None, :] % 2 == 0, np.cos(angle), np.sin(angle)).astype(np.float32)


def split_table(table):
    high = table.astype(ml_dtypes.bfloat16)
    low = (table - high.astype(np.float32)).astype(ml_dtypes.bfloat16)
    return np.concatenate([high, high, low], axis=1)


def table_dot(parts, value):
    high = value.astype(jnp.bfloat16)
    low = (value - high.astype(jnp.float32)).astype(jnp.bfloat16)
    return jnp.dot(
        parts, jnp.concatenate([high, low, high], axis=0), preferred_element_type=jnp.float32
    )


def f32(*shape):
    return jax.ShapeDtypeStruct(shape, jnp.float32)


TOKEN = f32(SUBLANES, LANES)


def call(kernel, out_shape, inputs, after=(), scratch=(), flops=0, smem=(0,), hbm=(), out_hbm=False, limit=LIMIT):
    count, tokens, made = len(inputs), len(after), len(out_shape)
    size = sum(4 * np.prod(x.shape) for x in (*inputs, *out_shape))

    def run(*refs):
        outs = refs[count + tokens : count + tokens + made]
        token, rest = refs[count + tokens + made], refs[count + tokens + made + 1 :]
        token[...] = jnp.zeros_like(token)
        kernel(*refs[:count], *outs, *rest)

    return pl.pallas_call(
        run,
        name=kernel.func.__name__,
        out_shape=[jax.ShapeDtypeStruct(x.shape, x.dtype) for x in (*out_shape, TOKEN)],
        in_specs=[SMEM if n in smem else HBM if n in hbm else VMEM for n in range(count)] + [VMEM] * tokens,
        out_specs=[HBM if out_hbm else VMEM] * made + [VMEM],
        scratch_shapes=list(scratch),
        compiler_params=pltpu.CompilerParams(vmem_limit_bytes=limit),
        cost_estimate=pl.CostEstimate(flops=flops, bytes_accessed=int(size), transcendentals=0),
    )(*inputs, *after)


def xor_permute(value, axis, step):
    count = lax.axis_size(axis)
    return lax.ppermute(value, axis, [(i, i ^ step) for i in range(count)])


def store_rows(block, row, spans, outs):
    turned = jnp.swapaxes(block, 0, 1)
    for r in range(SUBLANES):
        for (first, length), out in zip(spans, outs):
            if first <= row + r < first + length:
                lane = (row + r - first) * LANES
                out[:, lane : lane + LANES] = turned[r]


def pack_kernel(parts, spans, together, place, x, *refs):
    outs, (staged, sems) = refs[:-2], refs[-2:]
    if together:
        outs = [out.at[i] for i in range(parts) for out in outs]
    share_rows = x.shape[2] // parts
    low = spans[0][0] // SUBLANES * SUBLANES
    copies = []
    for i in range(parts):
        part = i if together else place[0] ^ i
        first = pl.multiple_of(part * share_rows + low, SUBLANES)
        copies.append(
            pltpu.make_async_copy(x.at[:, :, pl.ds(first, staged.shape[3]), :], staged.at[i], sems.at[i])
        )
        copies[i].start()
    for i in range(parts):
        copies[i].wait()
        for comp in range(2):
            for row in range(0, staged.shape[3], SUBLANES):
                store_rows(
                    staged[i, :, comp, row : row + SUBLANES, :],
                    low + row,
                    spans,
                    [out.at[comp] for out in outs[i * len(spans) : (i + 1) * len(spans)]],
                )


def head_kernel(parts, spans, together, place, x, shifts, offsets, *refs):
    outs = refs[: parts * len(spans)]
    pack_kernel(parts, spans, together, place, x, *refs)
    rows = shifts.shape[0]
    row = lax.broadcasted_iota(jnp.int32, (rows, LANES), 0)
    lane = lax.broadcasted_iota(jnp.int32, (rows, LANES), 1)
    plan = jnp.zeros((rows, LANES), jnp.int32)
    for j in range(rows):
        numbers = jnp.where(lane == 0, shifts[j], jnp.where(lane == 1, offsets[0, j], offsets[1, j]))
        plan = jnp.where(row == j, numbers, plan)
    for i in range(parts):
        outs[i * len(spans)][2, :, :LANES] = plan.astype(jnp.float32)


def seen_kernel(place, *pieces):
    pass


def gather_kernel(parts, together, place, *refs):
    if together:
        pieces, outs = [refs[0].at[q] for q in range(parts)], refs[1:]
    else:
        pieces, outs = refs[:parts], refs[parts:]
    rows = pieces[0].shape[1]
    for i in range(parts):
        first = i * rows if together else pl.multiple_of((place[0] ^ i) * rows, rows)
        lane = 0
        for out in outs:
            out[:, pl.ds(first, rows), :] = pieces[i][:2, :, lane : lane + out.shape[2]]
            lane += out.shape[2]


def head_gather_kernel(parts, place, *refs):
    pieces, (own, plan) = refs[:parts], refs[parts:]
    gather_kernel(parts, False, place, *pieces, own)
    rows = pieces[0].shape[1]
    for i in range(parts):
        first = pl.multiple_of((place[0] ^ i) * rows, rows)
        numbers = pieces[i][2, :, :LANES].astype(jnp.int32)
        for n in range(3):
            plan[n, pl.ds(first, rows), :] = jnp.broadcast_to(numbers[:, n : n + 1], (rows, LANES))


def in_first(me, base, size, shifts):
    offset = (me - base + 1 + shifts) & (2 * size - 1)
    return ((base - 1 - shifts + offset - me) & (4 * size - 1)) == 0


def choose(me, size, shifts):
    clear = ~(size - 1)
    kept = in_first(me, me & clear, size, shifts)
    sent = in_first(me, (me ^ size) & clear, size, shifts)
    return kept, sent


def is_outer(me, count):
    return ((me // (count // 2)) ^ (me // (count // 4))) & 1 == 0


def sample_step(count, place, table, shifts, own, far, send, keep):
    me = place[1]
    kept, sent = choose(me, count // 4, shifts[0])
    parts = table[...]
    for comp in range(2):
        near_samples = table_dot(parts, own[comp])
        far_samples = table_dot(parts, far[comp, :, : own.shape[2]])
        for lane in range(0, own.shape[2], LANES):
            here = slice(lane, lane + LANES)
            keep[comp, :, here] = jnp.where(kept, near_samples[:, here], far_samples[:, here])
            send[comp, :, here] = jnp.where(sent, near_samples[:, here], far_samples[:, here])


def copy_lanes(source, target):
    width = min(source.shape[2], target.shape[2])
    target[:, :, :width] = source[:, :, :width]


def first_kernel(count, place, table, shifts, own, arrived, following, send, keep):
    outer = is_outer(place[1], count)

    @pl.when(outer)
    def _():
        copy_lanes(following, send)
        keep[...] = own[...]

    @pl.when(jnp.logical_not(outer))
    def _():
        sample_step(count, place, table, shifts, own, arrived, send, keep)


def second_kernel(count, place, table, shifts, own, arrived, following, kept, send, keep):
    outer = is_outer(place[1], count)

    @pl.when(outer)
    def _():
        sample_step(count, place, table, shifts, own, arrived, send, keep)

    @pl.when(jnp.logical_not(outer))
    def _():
        copy_lanes(following, send)
        keep[...] = kept[...]


def middle_kernel(count, size, place, shifts, first, slot_a, slot_b, send, keep):
    me = place[1]
    outer = is_outer(me, count)
    kept, sent = choose(me, size, shifts[0])
    for comp in range(2):
        for lane in range(0, first.shape[2], LANES):
            here = slice(lane, lane + LANES)
            one = first[comp, :, here]
            two = jnp.where(outer, slot_a[comp, :, here], slot_b[comp, :, here])
            keep[comp, :, here] = jnp.where(kept, one, two)
            send[comp, :, here] = jnp.where(sent, one, two)


def pair_kernel(count, place, keep, slot_a, slot_b, pair):
    outer = is_outer(place[1], count)
    pair[0:2] = keep[...]

    @pl.when(outer)
    def _():
        pair[2:4] = slot_a[:, :, : pair.shape[2]]

    @pl.when(jnp.logical_not(outer))
    def _():
        pair[2:4] = slot_b[:, :, : pair.shape[2]]


def flux_kernel(parts, together, chunks, row0, place, table, plan, iron, weights, *refs):
    pairs, fars = refs[:chunks], refs[chunks : 2 * chunks]
    flux, result = refs[-2:]
    outs = [refs[2 * chunks].at[q] for q in range(parts)] if together else refs[2 * chunks : -2]
    total = outs[0].shape[2]
    tm, me = place[0], place[1]
    source = [((me + plan[1 + m] - plan[0]) ^ me) & 3 for m in range(2)]
    is_near = [s == 0 for s in source]
    is_two = [s == 2 for s in source]
    is_one = [s == 1 for s in source]
    quarter = tm * (iron.shape[0] // parts) + row0
    lane = 0
    for k in range(chunks):
        for inner in range(0, pairs[k].shape[2], LANES):
            here = slice(inner, inner + LANES)
            there = slice(row0 * LANES + lane, row0 * LANES + lane + LANES)
            field = []
            for comp in range(2):
                blocks = [ref[c, :, here] for ref in (pairs[k], fars[k]) for c in (comp, 2 + comp)]
                terms = [
                    weights[m, :, there]
                    * jnp.where(
                        is_near[m],
                        blocks[0],
                        jnp.where(is_two[m], blocks[1], jnp.where(is_one[m], blocks[2], blocks[3])),
                    )
                    for m in range(2)
                ]
                field.append(terms[0] + terms[1])
            square = field[0] * field[0] + field[1] * field[1]
            gain = iron[pl.ds(quarter + lane // LANES, 1), :] * (1.0 + square / (1.0 + square))
            for comp in range(2):
                flux[:, comp * total + lane : comp * total + lane + LANES] = gain * field[comp]
            lane += LANES
    result[...] = table_dot(table[...], flux[...])
    rows = result.shape[0] // parts
    for i in range(parts):
        first = i * rows if together else pl.multiple_of((tm ^ i) * rows, rows)
        for comp in range(2):
            outs[i][comp] = result[pl.ds(first, rows), comp * total : (comp + 1) * total]


def finish_kernel(parts, together, groups, place, source, *refs):
    pieces, (out, made, sems) = refs[:-3], refs[-3:]
    if together:
        pieces = [piece.at[q] for piece in pieces for q in range(parts)]
    share_rows = source.shape[2] // parts
    copies = []
    for i in range(parts):
        first = pl.multiple_of((i if together else place[0] ^ i) * share_rows, SUBLANES)
        for comp in range(2):
            rows = [
                pieces[g * parts + i][comp, :, lane : lane + LANES]
                for g in range(groups)
                for lane in range(0, pieces[g * parts].shape[2], LANES)
            ]
            for row in range(0, share_rows, SUBLANES):
                turned = jnp.swapaxes(jnp.stack(rows[row : row + SUBLANES]), 0, 1)
                made[i, :, comp, row : row + SUBLANES, :] = turned - source[:, comp, pl.ds(first + row, SUBLANES), :]
        copies.append(
            pltpu.make_async_copy(made.at[i], out.at[:, :, pl.ds(first, share_rows), :], sems.at[i])
        )
        copies[i].start()
    for copy in copies:
        copy.wait()


def body(rotor_coeffs, mortar_weights, block_shifts, stencil_offsets, reluctivity, source):
    parts, count = lax.axis_size("tm"), lax.axis_size("azim")
    coeff_rows, comps, _, nodes = rotor_coeffs.shape
    sample_rows = mortar_weights.shape[0]
    coeffs, samples = coeff_rows * parts, sample_rows * parts
    share_rows = nodes // parts // LANES
    bounds = np.cumsum((0,) + CHUNK_SHARES) * share_rows // sum(CHUNK_SHARES)
    heights = [int(h) for h in np.diff(bounds)]
    widths = [h * LANES for h in heights]
    chunks = len(heights)
    place = jnp.stack([lax.axis_index("tm"), lax.axis_index("azim")]).astype(jnp.int32)
    table = basis_table(samples, coeffs)
    forward = jnp.asarray(split_table(table))
    backward = jnp.asarray(split_table(np.ascontiguousarray(table.T) * np.float32(2.0 / samples)))
    gates = {}

    def in_rows(x):
        return x.reshape(x.shape[0], comps, nodes // LANES, LANES)

    def pack(x, spans, after=(), plan=(), together=False):
        low = spans[0][0] // SUBLANES * SUBLANES
        high = -(-(spans[-1][0] + spans[-1][1]) // SUBLANES) * SUBLANES
        shape = (3 if plan else 2, x.shape[0], spans[0][1] * LANES)
        *outs, token = call(
            functools.partial(head_kernel if plan else pack_kernel, parts, spans, together),
            [f32(parts, *shape)] if together else [f32(*shape)] * parts,
            (place, in_rows(x), *plan),
            after=after,
            scratch=(
                pltpu.VMEM((parts, x.shape[0], comps, high - low, LANES), jnp.float32),
                pltpu.SemaphoreType.DMA((parts,)),
            ),
            smem=(0, 2, 3) if plan else (0,),
            hbm=(1,),
            limit=FULL if plan else LIMIT,
        )
        return outs, token

    def swap(pieces):
        if len(pieces) == 1:
            return [lax.all_to_all(pieces[0], "tm", split_axis=0, concat_axis=0, tiled=True)]
        return [pieces[0]] + [xor_permute(pieces[i], "tm", i) for i in range(1, parts)]

    def gather(pieces, lanes, rows, after=()):
        *outs, token = call(
            functools.partial(gather_kernel, parts, len(pieces) == 1),
            [f32(2, rows, w) for w in lanes],
            (place, *pieces),
            after=after,
        )
        return outs, token

    head, token = pack(rotor_coeffs, [(0, heights[0])], plan=(block_shifts, stencil_offsets.T))
    rest_span = [(heights[0], share_rows - heights[0])]
    if REST_FIRST:
        rest, token = pack(rotor_coeffs, rest_span, after=(token,), together=REST_TOGETHER)
    own_first, plan, token = call(
        functools.partial(head_gather_kernel, parts),
        [f32(2, coeffs, widths[0]), jax.ShapeDtypeStruct((3, samples, LANES), jnp.int32)],
        (place, *swap(head)),
        after=(token,) if REST_FIRST else (),
    )
    if not REST_FIRST:
        rest, token = pack(rotor_coeffs, rest_span, after=(token,), together=REST_TOGETHER)
    own_rest, token = gather(swap(rest), widths[1:], coeffs, (token,))
    own = [own_first] + own_rest
    weights, token = pack(mortar_weights, [(0, share_rows)], after=(token,), together=WEIGHTS_TOGETHER)
    gates[PACK_GATE] = [token]
    (weights,), token = gather(swap(weights), [share_rows * LANES], samples)
    gates.setdefault(WEIGHT_GATE, []).append(token)

    half, fourth = count // 2, count // 4
    outer = [d for d in range(count) if is_outer(d, count)]
    inner = [d for d in range(count) if not is_outer(d, count)]
    coeff_a = [(d, d ^ half) for d in outer]
    coeff_b = [(d, d ^ half) for d in inner]
    sample_a = [(d, d ^ fourth) for d in inner]
    sample_b = [(d, d ^ fourth) for d in outer]

    def neighbours(keep, slot_a, slot_b, after):
        size = count // 8
        while size >= 2:
            send, keep, _ = call(
                functools.partial(middle_kernel, count, size), [keep, keep], (place, plan, keep, slot_a, slot_b)
            )
            slot_a = slot_b = xor_permute(send, "azim", size)
            size //= 2
        pair, token = call(
            functools.partial(pair_kernel, count),
            [f32(4, samples, keep.shape[2])],
            (place, keep, slot_a, slot_b),
            after=after,
        )
        return pair, xor_permute(pair, "azim", 1), token

    iron = reluctivity.reshape(nodes // LANES, LANES)

    def flux(group, pairs):
        total = sum(widths[k] for k in group)
        *made, token = call(
            functools.partial(flux_kernel, parts, RESULTS_TOGETHER, len(group), sum(heights[: group[0]])),
            [f32(parts, 2, coeff_rows, total)] if RESULTS_TOGETHER else [f32(2, coeff_rows, total)] * parts,
            (place, backward, plan, iron, weights, *[pairs[k][0] for k in group], *[pairs[k][1] for k in group]),
            scratch=(pltpu.VMEM((samples, 2 * total), jnp.float32), pltpu.VMEM((coeffs, 2 * total), jnp.float32)),
            flops=4 * samples * 3 * coeffs * total,
        )
        return swap(made), token

    slots_a, slots_b, keeps, pairs, pieces = [], [], [], [], []
    send_a = send_b = own[0]
    for k in range(chunks):
        slots_a.append(lax.ppermute(send_a, "azim", coeff_a + (sample_a if k else [])))
        slots_b.append(lax.ppermute(send_b, "azim", coeff_b + (sample_b if k else [])))
        after = own[k + 1] if k + 1 < chunks else own[k]
        block, sent = f32(2, samples, widths[k]), f32(2, samples, max(widths[k], after.shape[2]))
        flops = 8 * samples * 3 * coeffs * widths[k]
        send_a, kept, _ = call(
            functools.partial(first_kernel, count),
            [sent, block],
            (place, forward, plan, own[k], slots_a[k], after),
            after=gates.get(k, ()),
            flops=flops,
        )
        send_b, kept, token = call(
            functools.partial(second_kernel, count),
            [sent, block],
            (place, forward, plan, own[k], slots_b[k], after, kept),
            flops=flops,
        )
        keeps.append(kept)
        if k:
            *pair, token = neighbours(keeps[k - 1], slots_a[k], slots_b[k], (token,) if PAIR_AFTER else ())
            gates.setdefault(k + PAIR_GATE, []).append(token)
            pairs.append(pair)
            for group in FLUX_GROUPS:
                if group[-1] == k - 1:
                    made, token = flux(group, pairs)
                    pieces += made
                    gates.setdefault(min(k + FLUX_GATE, chunks), []).append(token)
                    if k + SEEN_GATE <= chunks:
                        (token,) = call(functools.partial(seen_kernel), [], (place, *made))
                        gates.setdefault(k + SEEN_GATE, []).append(token)
    slot_a = lax.ppermute(send_a, "azim", sample_a)
    slot_b = lax.ppermute(send_b, "azim", sample_b)
    *pair, _ = neighbours(keeps[-1], slot_a, slot_b, gates.get(chunks, ()))
    pairs.append(pair)
    pieces += flux(FLUX_GROUPS[-1], pairs)[0]
    out, _ = call(
        functools.partial(finish_kernel, parts, RESULTS_TOGETHER, len(FLUX_GROUPS)),
        [f32(coeff_rows, comps, nodes // LANES, LANES)],
        (place, in_rows(source), *pieces),
        scratch=(
            pltpu.VMEM((parts, coeff_rows, comps, share_rows, LANES), jnp.float32),
            pltpu.SemaphoreType.DMA((parts,)),
        ),
        out_hbm=True,
    )
    return out.reshape(source.shape)


def solution(mesh):
    wide = P("tm", None, "azim", None)
    in_specs = (wide, wide, P("tm"), P("tm", None), P("azim", None), wide)
    return jax.shard_map(body, mesh=mesh, in_specs=in_specs, out_specs=wide, check_vma=False)
```

```python
import functools

import jax
import jax.numpy as jnp
import ml_dtypes
import numpy as np
from jax import lax
from jax.experimental import pallas as pl
from jax.experimental.pallas import tpu as pltpu
from jax.sharding import PartitionSpec as P

LANES = 128
CHUNK_SHARES = (8, 8, 8, 8)
FLUX_GROUPS = ((0,), (1,), (2,), (3,))
WEIGHTS_TOGETHER = False
RESULTS_TOGETHER = False
REST_TOGETHER = False
RELEASE = 2
PAIR_AFTER = True
PAIR_GATE = 1
FLUX_GATE = 2
SEEN_GATE = 2
SEEN_GROUPS = (0, 1)
TAIL_PAIR = 0
PACK_GATE = 1
WEIGHT_GATE = 3
REST_FIRST = True
HEAD_LIMIT = True
VMEM = pl.BlockSpec(memory_space=pltpu.VMEM)
SMEM = pl.BlockSpec(memory_space=pltpu.SMEM)
HBM = pl.BlockSpec(memory_space=pltpu.HBM)
SUBLANES = 8
LIMIT = 48 * 1024 * 1024
FULL = 62 * 1024 * 1024


def basis_table(sample_count, coefficient_count):
    column = np.arange(coefficient_count)
    order = 2 * (column // 2) + 1
    phase = order[None, :] * (2 * np.arange(sample_count)[:, None] + 1) % (4 * sample_count)
    angle = phase * (np.pi / (2 * sample_count))
    return np.where(column[None, :] % 2 == 0, np.cos(angle), np.sin(angle)).astype(np.float32)


def split_table(table):
    high = table.astype(ml_dtypes.bfloat16)
    low = (table - high.astype(np.float32)).astype(ml_dtypes.bfloat16)
    return np.concatenate([high, high, low], axis=1)


def table_dot(parts, value):
    high = value.astype(jnp.bfloat16)
    low = (value - high.astype(jnp.float32)).astype(jnp.bfloat16)
    return jnp.dot(
        parts, jnp.concatenate([high, low, high], axis=0), preferred_element_type=jnp.float32
    )


def f32(*shape):
    return jax.ShapeDtypeStruct(shape, jnp.float32)


TOKEN = f32(SUBLANES, LANES)


def call(kernel, out_shape, inputs, after=(), scratch=(), flops=0, smem=(0,), hbm=(), out_hbm=False, limit=LIMIT):
    count, tokens, made = len(inputs), len(after), len(out_shape)
    size = sum(4 * np.prod(x.shape) for x in (*inputs, *out_shape))

    def run(*refs):
        outs = refs[count + tokens : count + tokens + made]
        token, rest = refs[count + tokens + made], refs[count + tokens + made + 1 :]
        token[...] = jnp.zeros_like(token)
        kernel(*refs[:count], *outs, *rest)

    return pl.pallas_call(
        run,
        name=kernel.func.__name__,
        out_shape=[jax.ShapeDtypeStruct(x.shape, x.dtype) for x in (*out_shape, TOKEN)],
        in_specs=[SMEM if n in smem else HBM if n in hbm else VMEM for n in range(count)] + [VMEM] * tokens,
        out_specs=[HBM if out_hbm else VMEM] * made + [VMEM],
        scratch_shapes=list(scratch),
        compiler_params=pltpu.CompilerParams(vmem_limit_bytes=limit),
        cost_estimate=pl.CostEstimate(flops=flops, bytes_accessed=int(size), transcendentals=0),
    )(*inputs, *after)


def xor_permute(value, axis, step):
    count = lax.axis_size(axis)
    return lax.ppermute(value, axis, [(i, i ^ step) for i in range(count)])


def store_rows(block, row, spans, outs):
    turned = jnp.swapaxes(block, 0, 1)
    for r in range(SUBLANES):
        for (first, length), out in zip(spans, outs):
            if first <= row + r < first + length:
                lane = (row + r - first) * LANES
                out[:, lane : lane + LANES] = turned[r]


def pack_kernel(parts, spans, together, place, x, *refs):
    outs, (staged, sems) = refs[:-2], refs[-2:]
    if together:
        outs = [out.at[i] for i in range(parts) for out in outs]
    share_rows = x.shape[2] // parts
    low = spans[0][0] // SUBLANES * SUBLANES
    copies = []
    for i in range(parts):
        part = i if together else place[0] ^ i
        first = pl.multiple_of(part * share_rows + low, SUBLANES)
        copies.append(
            pltpu.make_async_copy(x.at[:, :, pl.ds(first, staged.shape[3]), :], staged.at[i], sems.at[i])
        )
        copies[i].start()
    for i in range(parts):
        copies[i].wait()
        for comp in range(2):
            for row in range(0, staged.shape[3], SUBLANES):
                store_rows(
                    staged[i, :, comp, row : row + SUBLANES, :],
                    low + row,
                    spans,
                    [out.at[comp] for out in outs[i * len(spans) : (i + 1) * len(spans)]],
                )


def head_kernel(parts, spans, together, place, x, shifts, offsets, *refs):
    outs = refs[: parts * len(spans)]
    pack_kernel(parts, spans, together, place, x, *refs)
    rows = shifts.shape[0]
    row = lax.broadcasted_iota(jnp.int32, (rows, LANES), 0)
    lane = lax.broadcasted_iota(jnp.int32, (rows, LANES), 1)
    plan = jnp.zeros((rows, LANES), jnp.int32)
    for j in range(rows):
        numbers = jnp.where(lane == 0, shifts[j], jnp.where(lane == 1, offsets[0, j], offsets[1, j]))
        plan = jnp.where(row == j, numbers, plan)
    for i in range(parts):
        out = outs[i * len(spans)]
        behind = spans[0][1] * LANES
        out[0, :, behind:] = plan.astype(jnp.float32)
        out[1, :, behind:] = jnp.zeros(plan.shape, jnp.float32)


def seen_kernel(place, *pieces):
    pass


def gather_kernel(parts, together, place, *refs):
    if together:
        pieces, outs = [refs[0].at[q] for q in range(parts)], refs[1:]
    else:
        pieces, outs = refs[:parts], refs[parts:]
    rows = pieces[0].shape[1]
    for i in range(parts):
        first = i * rows if together else pl.multiple_of((place[0] ^ i) * rows, rows)
        lane = 0
        for out in outs:
            out[:, pl.ds(first, rows), :] = pieces[i][:, :, lane : lane + out.shape[2]]
            lane += out.shape[2]


def head_gather_kernel(parts, place, *refs):
    pieces, (own, plan) = refs[:parts], refs[parts:]
    gather_kernel(parts, False, place, *pieces, own)
    rows = pieces[0].shape[1]
    for i in range(parts):
        first = pl.multiple_of((place[0] ^ i) * rows, rows)
        numbers = pieces[i][0, :, own.shape[2] :].astype(jnp.int32)
        for n in range(3):
            plan[n, pl.ds(first, rows), :] = jnp.broadcast_to(numbers[:, n : n + 1], (rows, LANES))


def in_first(me, base, size, shifts):
    offset = (me - base + 1 + shifts) & (2 * size - 1)
    return ((base - 1 - shifts + offset - me) & (4 * size - 1)) == 0


def choose(me, size, shifts):
    clear = ~(size - 1)
    kept = in_first(me, me & clear, size, shifts)
    sent = in_first(me, (me ^ size) & clear, size, shifts)
    return kept, sent


def is_outer(me, count):
    return ((me // (count // 2)) ^ (me // (count // 4))) & 1 == 0


def sample_step(count, place, table, shifts, own, far, send, keep):
    me = place[1]
    kept, sent = choose(me, count // 4, shifts[0])
    parts = table[...]
    for comp in range(2):
        near_samples = table_dot(parts, own[comp])
        far_samples = table_dot(parts, far[comp, :, : own.shape[2]])
        for lane in range(0, own.shape[2], LANES):
            here = slice(lane, lane + LANES)
            keep[comp, :, here] = jnp.where(kept, near_samples[:, here], far_samples[:, here])
            send[comp, :, here] = jnp.where(sent, near_samples[:, here], far_samples[:, here])


def copy_lanes(source, target):
    width = min(source.shape[2], target.shape[2])
    target[:, :, :width] = source[:, :, :width]


def first_kernel(count, place, table, shifts, own, arrived, following, send, keep):
    outer = is_outer(place[1], count)

    @pl.when(outer)
    def _():
        copy_lanes(following, send)
        keep[...] = own[...]

    @pl.when(jnp.logical_not(outer))
    def _():
        sample_step(count, place, table, shifts, own, arrived, send, keep)


def second_kernel(count, place, table, shifts, own, arrived, following, kept, send, keep):
    outer = is_outer(place[1], count)

    @pl.when(outer)
    def _():
        sample_step(count, place, table, shifts, own, arrived, send, keep)

    @pl.when(jnp.logical_not(outer))
    def _():
        copy_lanes(following, send)
        keep[...] = kept[...]


def middle_kernel(count, size, place, shifts, first, slot_a, slot_b, send, keep):
    me = place[1]
    outer = is_outer(me, count)
    kept, sent = choose(me, size, shifts[0])
    for comp in range(2):
        for lane in range(0, first.shape[2], LANES):
            here = slice(lane, lane + LANES)
            one = first[comp, :, here]
            two = jnp.where(outer, slot_a[comp, :, here], slot_b[comp, :, here])
            keep[comp, :, here] = jnp.where(kept, one, two)
            send[comp, :, here] = jnp.where(sent, one, two)


def pair_kernel(count, place, keep, slot_a, slot_b, pair):
    outer = is_outer(place[1], count)
    pair[0:2] = keep[...]

    @pl.when(outer)
    def _():
        pair[2:4] = slot_a[:, :, : pair.shape[2]]

    @pl.when(jnp.logical_not(outer))
    def _():
        pair[2:4] = slot_b[:, :, : pair.shape[2]]


def flux_kernel(parts, together, chunks, row0, place, table, plan, iron, weights, *refs):
    pairs, fars = refs[:chunks], refs[chunks : 2 * chunks]
    flux, result = refs[-2:]
    outs = [refs[2 * chunks].at[q] for q in range(parts)] if together else refs[2 * chunks : -2]
    total = outs[0].shape[2]
    tm, me = place[0], place[1]
    source = [((me + plan[1 + m] - plan[0]) ^ me) & 3 for m in range(2)]
    is_near = [s == 0 for s in source]
    is_two = [s == 2 for s in source]
    is_one = [s == 1 for s in source]
    quarter = tm * (iron.shape[0] // parts) + row0
    lane = 0
    for k in range(chunks):
        for inner in range(0, pairs[k].shape[2], LANES):
            here = slice(inner, inner + LANES)
            there = slice(row0 * LANES + lane, row0 * LANES + lane + LANES)
            field = []
            for comp in range(2):
                blocks = [ref[c, :, here] for ref in (pairs[k], fars[k]) for c in (comp, 2 + comp)]
                terms = [
                    weights[m, :, there]
                    * jnp.where(
                        is_near[m],
                        blocks[0],
                        jnp.where(is_two[m], blocks[1], jnp.where(is_one[m], blocks[2], blocks[3])),
                    )
                    for m in range(2)
                ]
                field.append(terms[0] + terms[1])
            square = field[0] * field[0] + field[1] * field[1]
            gain = iron[pl.ds(quarter + lane // LANES, 1), :] * (1.0 + square / (1.0 + square))
            for comp in range(2):
                flux[:, comp * total + lane : comp * total + lane + LANES] = gain * field[comp]
            lane += LANES
    result[...] = table_dot(table[...], flux[...])
    rows = result.shape[0] // parts
    for i in range(parts):
        first = i * rows if together else pl.multiple_of((tm ^ i) * rows, rows)
        for comp in range(2):
            outs[i][comp] = result[pl.ds(first, rows), comp * total : (comp + 1) * total]


def finish_kernel(parts, together, groups, place, source, *refs):
    pieces, (out, made, sems) = refs[:-3], refs[-3:]
    if together:
        pieces = [piece.at[q] for piece in pieces for q in range(parts)]
    share_rows = source.shape[2] // parts
    copies = []
    for i in range(parts):
        first = pl.multiple_of((i if together else place[0] ^ i) * share_rows, SUBLANES)
        for comp in range(2):
            rows = [
                pieces[g * parts + i][comp, :, lane : lane + LANES]
                for g in range(groups)
                for lane in range(0, pieces[g * parts].shape[2], LANES)
            ]
            for row in range(0, share_rows, SUBLANES):
                turned = jnp.swapaxes(jnp.stack(rows[row : row + SUBLANES]), 0, 1)
                made[i, :, comp, row : row + SUBLANES, :] = turned - source[:, comp, pl.ds(first + row, SUBLANES), :]
        copies.append(
            pltpu.make_async_copy(made.at[i], out.at[:, :, pl.ds(first, share_rows), :], sems.at[i])
        )
        copies[i].start()
    for copy in copies:
        copy.wait()


def body(rotor_coeffs, mortar_weights, block_shifts, stencil_offsets, reluctivity, source):
    parts, count = lax.axis_size("tm"), lax.axis_size("azim")
    coeff_rows, comps, _, nodes = rotor_coeffs.shape
    sample_rows = mortar_weights.shape[0]
    coeffs, samples = coeff_rows * parts, sample_rows * parts
    share_rows = nodes // parts // LANES
    bounds = np.cumsum((0,) + CHUNK_SHARES) * share_rows // sum(CHUNK_SHARES)
    heights = [int(h) for h in np.diff(bounds)]
    widths = [h * LANES for h in heights]
    chunks = len(heights)
    place = jnp.stack([lax.axis_index("tm"), lax.axis_index("azim")]).astype(jnp.int32)
    table = basis_table(samples, coeffs)
    forward = jnp.asarray(split_table(table))
    backward = jnp.asarray(split_table(np.ascontiguousarray(table.T) * np.float32(2.0 / samples)))
    gates = {}

    def in_rows(x):
        return x.reshape(x.shape[0], comps, nodes // LANES, LANES)

    def pack(x, spans, after=(), plan=(), together=False):
        low = spans[0][0] // SUBLANES * SUBLANES
        high = -(-(spans[-1][0] + spans[-1][1]) // SUBLANES) * SUBLANES
        shape = (2, x.shape[0], (spans[0][1] + bool(plan)) * LANES)
        *outs, token = call(
            functools.partial(head_kernel if plan else pack_kernel, parts, spans, together),
            [f32(parts, *shape)] if together else [f32(*shape)] * parts,
            (place, in_rows(x), *plan),
            after=after,
            scratch=(
                pltpu.VMEM((parts, x.shape[0], comps, high - low, LANES), jnp.float32),
                pltpu.SemaphoreType.DMA((parts,)),
            ),
            smem=(0, 2, 3) if plan else (0,),
            hbm=(1,),
            limit=FULL if plan else LIMIT,
        )
        return outs, token

    def swap(pieces):
        if len(pieces) == 1:
            return [lax.all_to_all(pieces[0], "tm", split_axis=0, concat_axis=0, tiled=True)]
        return [pieces[0]] + [xor_permute(pieces[i], "tm", i) for i in range(1, parts)]

    def gather(pieces, lanes, rows, after=()):
        *outs, token = call(
            functools.partial(gather_kernel, parts, len(pieces) == 1),
            [f32(2, rows, w) for w in lanes],
            (place, *pieces),
            after=after,
        )
        return outs, token

    head, token = pack(rotor_coeffs, [(0, heights[0])], plan=(block_shifts, stencil_offsets.T))
    rest_span = [(heights[0], share_rows - heights[0])]
    if REST_FIRST:
        rest, token = pack(rotor_coeffs, rest_span, after=(token,), together=REST_TOGETHER)
    own_first, plan, token = call(
        functools.partial(head_gather_kernel, parts),
        [f32(2, coeffs, widths[0]), jax.ShapeDtypeStruct((3, samples, LANES), jnp.int32)],
        (place, *swap(head)),
        after=(token,) if REST_FIRST else (),
    )
    if not REST_FIRST:
        rest, token = pack(rotor_coeffs, rest_span, after=(token,), together=REST_TOGETHER)
    own_rest, token = gather(swap(rest), widths[1:], coeffs, (token,))
    own = [own_first] + own_rest
    weights, token = pack(mortar_weights, [(0, share_rows)], after=(token,), together=WEIGHTS_TOGETHER)
    gates[PACK_GATE] = [token]
    (weights,), token = gather(swap(weights), [share_rows * LANES], samples)
    gates.setdefault(WEIGHT_GATE, []).append(token)

    half, fourth = count // 2, count // 4
    outer = [d for d in range(count) if is_outer(d, count)]
    inner = [d for d in range(count) if not is_outer(d, count)]
    coeff_a = [(d, d ^ half) for d in outer]
    coeff_b = [(d, d ^ half) for d in inner]
    sample_a = [(d, d ^ fourth) for d in inner]
    sample_b = [(d, d ^ fourth) for d in outer]

    def neighbours(keep, slot_a, slot_b, after):
        size = count // 8
        while size >= 2:
            send, keep, _ = call(
                functools.partial(middle_kernel, count, size), [keep, keep], (place, plan, keep, slot_a, slot_b)
            )
            slot_a = slot_b = xor_permute(send, "azim", size)
            size //= 2
        pair, token = call(
            functools.partial(pair_kernel, count),
            [f32(4, samples, keep.shape[2])],
            (place, keep, slot_a, slot_b),
            after=after,
        )
        return pair, xor_permute(pair, "azim", 1), token

    iron = reluctivity.reshape(nodes // LANES, LANES)

    def flux(group, pairs):
        total = sum(widths[k] for k in group)
        *made, token = call(
            functools.partial(flux_kernel, parts, RESULTS_TOGETHER, len(group), sum(heights[: group[0]])),
            [f32(parts, 2, coeff_rows, total)] if RESULTS_TOGETHER else [f32(2, coeff_rows, total)] * parts,
            (place, backward, plan, iron, weights, *[pairs[k][0] for k in group], *[pairs[k][1] for k in group]),
            scratch=(pltpu.VMEM((samples, 2 * total), jnp.float32), pltpu.VMEM((coeffs, 2 * total), jnp.float32)),
            flops=4 * samples * 3 * coeffs * total,
        )
        return swap(made), token

    slots_a, slots_b, keeps, pairs, pieces = [], [], [], [], []
    send_a = send_b = own[0]
    for k in range(chunks):
        slots_a.append(lax.ppermute(send_a, "azim", coeff_a + (sample_a if k else [])))
        slots_b.append(lax.ppermute(send_b, "azim", coeff_b + (sample_b if k else [])))
        after = own[k + 1] if k + 1 < chunks else own[k]
        block, sent = f32(2, samples, widths[k]), f32(2, samples, max(widths[k], after.shape[2]))
        flops = 8 * samples * 3 * coeffs * widths[k]
        send_a, kept, _ = call(
            functools.partial(first_kernel, count),
            [sent, block],
            (place, forward, plan, own[k], slots_a[k], after),
            after=gates.get(k, ()),
            flops=flops,
        )
        send_b, kept, token = call(
            functools.partial(second_kernel, count),
            [sent, block],
            (place, forward, plan, own[k], slots_b[k], after, kept),
            flops=flops,
        )
        keeps.append(kept)
        if k:
            *pair, token = neighbours(keeps[k - 1], slots_a[k], slots_b[k], (token,) if PAIR_AFTER else ())
            gates.setdefault(k + PAIR_GATE, []).append(token)
            pairs.append(pair)
            for group in FLUX_GROUPS:
                if group[-1] == k - 1:
                    made, token = flux(group, pairs)
                    pieces += made
                    gates.setdefault(min(k + FLUX_GATE, chunks), []).append(token)
                    if group[-1] in SEEN_GROUPS:
                        (token,) = call(functools.partial(seen_kernel), [], (place, *made))
                        gates.setdefault(min(k + SEEN_GATE, chunks), []).append(token)
    slot_a = lax.ppermute(send_a, "azim", sample_a)
    slot_b = lax.ppermute(send_b, "azim", sample_b)
    *pair, _ = neighbours(keeps[-1], slot_a, slot_b, gates.get(chunks, ()))
    pairs.append(pair)
    pieces += flux(FLUX_GROUPS[-1], pairs)[0]
    out, _ = call(
        functools.partial(finish_kernel, parts, RESULTS_TOGETHER, len(FLUX_GROUPS)),
        [f32(coeff_rows, comps, nodes // LANES, LANES)],
        (place, in_rows(source), *pieces),
        scratch=(
            pltpu.VMEM((parts, coeff_rows, comps, share_rows, LANES), jnp.float32),
            pltpu.SemaphoreType.DMA((parts,)),
        ),
        out_hbm=True,
    )
    return out.reshape(source.shape)


def solution(mesh):
    wide = P("tm", None, "azim", None)
    in_specs = (wide, wide, P("tm"), P("tm", None), P("azim", None), wide)
    return jax.shard_map(body, mesh=mesh, in_specs=in_specs, out_specs=wide, check_vma=False)
```

```python
import functools

import jax
import jax.numpy as jnp
import ml_dtypes
import numpy as np
from jax import lax
from jax.experimental import pallas as pl
from jax.experimental.pallas import tpu as pltpu
from jax.sharding import PartitionSpec as P

LANES = 128
CHUNK_SHARES = (8, 8, 8, 8)
FLUX_GATE = 3
SEEN = (0, 1)
VMEM = pl.BlockSpec(memory_space=pltpu.VMEM)
SMEM = pl.BlockSpec(memory_space=pltpu.SMEM)
HBM = pl.BlockSpec(memory_space=pltpu.HBM)
SUBLANES = 8
LIMIT = 48 * 1024 * 1024
FULL = 62 * 1024 * 1024


def basis_table(sample_count, coefficient_count):
    column = np.arange(coefficient_count)
    order = 2 * (column // 2) + 1
    phase = order[None, :] * (2 * np.arange(sample_count)[:, None] + 1) % (4 * sample_count)
    angle = phase * (np.pi / (2 * sample_count))
    return np.where(column[None, :] % 2 == 0, np.cos(angle), np.sin(angle)).astype(np.float32)


def split_table(table):
    high = table.astype(ml_dtypes.bfloat16)
    low = (table - high.astype(np.float32)).astype(ml_dtypes.bfloat16)
    return np.concatenate([high, high, low], axis=1)


def table_dot(parts, value):
    high = value.astype(jnp.bfloat16)
    low = (value - high.astype(jnp.float32)).astype(jnp.bfloat16)
    return jnp.dot(
        parts, jnp.concatenate([high, low, high], axis=0), preferred_element_type=jnp.float32
    )


def f32(*shape):
    return jax.ShapeDtypeStruct(shape, jnp.float32)


TOKEN = f32(SUBLANES, LANES)


def call(kernel, out_shape, inputs, after=(), scratch=(), flops=0, smem=(0,), hbm=(), out_hbm=False, limit=LIMIT):
    count, tokens, made = len(inputs), len(after), len(out_shape)
    size = sum(4 * np.prod(x.shape) for x in (*inputs, *out_shape))

    def run(*refs):
        outs = refs[count + tokens : count + tokens + made]
        token, rest = refs[count + tokens + made], refs[count + tokens + made + 1 :]
        token[...] = jnp.zeros_like(token)
        kernel(*refs[:count], *outs, *rest)

    return pl.pallas_call(
        run,
        name=kernel.func.__name__,
        out_shape=[jax.ShapeDtypeStruct(x.shape, x.dtype) for x in (*out_shape, TOKEN)],
        in_specs=[SMEM if n in smem else HBM if n in hbm else VMEM for n in range(count)] + [VMEM] * tokens,
        out_specs=[HBM if out_hbm else VMEM] * made + [VMEM],
        scratch_shapes=list(scratch),
        compiler_params=pltpu.CompilerParams(vmem_limit_bytes=limit),
        cost_estimate=pl.CostEstimate(flops=flops, bytes_accessed=int(size), transcendentals=0),
    )(*inputs, *after)


def xor_permute(value, axis, step):
    count = lax.axis_size(axis)
    return lax.ppermute(value, axis, [(i, i ^ step) for i in range(count)])


def store_rows(block, row, spans, outs):
    turned = jnp.swapaxes(block, 0, 1)
    for r in range(SUBLANES):
        for (first, length), out in zip(spans, outs):
            if first <= row + r < first + length:
                lane = (row + r - first) * LANES
                out[:, lane : lane + LANES] = turned[r]


def pack_kernel(parts, spans, place, x, *refs):
    outs, (staged, sems) = refs[:-2], refs[-2:]
    share_rows = x.shape[2] // parts
    low = spans[0][0] // SUBLANES * SUBLANES
    copies = []
    for i in range(parts):
        first = pl.multiple_of((place[0] ^ i) * share_rows + low, SUBLANES)
        copies.append(
            pltpu.make_async_copy(x.at[:, :, pl.ds(first, staged.shape[3]), :], staged.at[i], sems.at[i])
        )
        copies[i].start()
    for i in range(parts):
        copies[i].wait()
        for comp in range(2):
            for row in range(0, staged.shape[3], SUBLANES):
                store_rows(
                    staged[i, :, comp, row : row + SUBLANES, :],
                    low + row,
                    spans,
                    [out.at[comp] for out in outs[i * len(spans) : (i + 1) * len(spans)]],
                )


def plan_pack_kernel(parts, spans, place, x, shifts, offsets, *refs):
    outs = refs[: parts * len(spans)]
    pack_kernel(parts, spans, place, x, *refs)
    rows = shifts.shape[0]
    row = lax.broadcasted_iota(jnp.int32, (rows, LANES), 0)
    lane = lax.broadcasted_iota(jnp.int32, (rows, LANES), 1)
    plan = jnp.zeros((rows, LANES), jnp.int32)
    for j in range(rows):
        numbers = jnp.where(lane == 0, shifts[j], jnp.where(lane == 1, offsets[0, j], offsets[1, j]))
        plan = jnp.where(row == j, numbers, plan)
    for i in range(parts):
        out = outs[i * len(spans)]
        behind = spans[0][1] * LANES
        out[0, :, behind:] = plan.astype(jnp.float32)
        out[1, :, behind:] = jnp.zeros(plan.shape, jnp.float32)


def seen_kernel(place, *pieces):
    pass


def gather_kernel(parts, place, *refs):
    pieces, outs = refs[:parts], refs[parts:]
    rows = pieces[0].shape[1]
    for i in range(parts):
        first = pl.multiple_of((place[0] ^ i) * rows, rows)
        lane = 0
        for out in outs:
            out[:, pl.ds(first, rows), :] = pieces[i][:, :, lane : lane + out.shape[2]]
            lane += out.shape[2]


def plan_gather_kernel(parts, place, *refs):
    pieces, (*outs, plan) = refs[:parts], refs[parts:]
    gather_kernel(parts, place, *pieces, *outs)
    rows = pieces[0].shape[1]
    behind = sum(out.shape[2] for out in outs)
    for i in range(parts):
        first = pl.multiple_of((place[0] ^ i) * rows, rows)
        numbers = pieces[i][0, :, behind:].astype(jnp.int32)
        for n in range(3):
            plan[n, pl.ds(first, rows), :] = jnp.broadcast_to(numbers[:, n : n + 1], (rows, LANES))


def in_first(me, base, size, shifts):
    offset = (me - base + 1 + shifts) & (2 * size - 1)
    return ((base - 1 - shifts + offset - me) & (4 * size - 1)) == 0


def choose(me, size, shifts):
    clear = ~(size - 1)
    kept = in_first(me, me & clear, size, shifts)
    sent = in_first(me, (me ^ size) & clear, size, shifts)
    return kept, sent


def is_outer(me, count):
    return ((me // (count // 2)) ^ (me // (count // 4))) & 1 == 0


def sample_step(count, place, table, shifts, own, far, send, keep):
    me = place[1]
    kept, sent = choose(me, count // 4, shifts[0])
    parts = table[...]
    for comp in range(2):
        near_samples = table_dot(parts, own[comp])
        far_samples = table_dot(parts, far[comp, :, : own.shape[2]])
        for lane in range(0, own.shape[2], LANES):
            here = slice(lane, lane + LANES)
            keep[comp, :, here] = jnp.where(kept, near_samples[:, here], far_samples[:, here])
            send[comp, :, here] = jnp.where(sent, near_samples[:, here], far_samples[:, here])


def copy_lanes(source, target):
    width = min(source.shape[2], target.shape[2])
    target[:, :, :width] = source[:, :, :width]


def first_kernel(count, place, table, shifts, own, arrived, following, send, keep):
    outer = is_outer(place[1], count)

    @pl.when(outer)
    def _():
        copy_lanes(following, send)
        keep[...] = own[...]

    @pl.when(jnp.logical_not(outer))
    def _():
        sample_step(count, place, table, shifts, own, arrived, send, keep)


def second_kernel(count, place, table, shifts, own, arrived, following, kept, send, keep):
    outer = is_outer(place[1], count)

    @pl.when(outer)
    def _():
        sample_step(count, place, table, shifts, own, arrived, send, keep)

    @pl.when(jnp.logical_not(outer))
    def _():
        copy_lanes(following, send)
        keep[...] = kept[...]


def middle_kernel(count, size, place, shifts, first, slot_a, slot_b, send, keep):
    me = place[1]
    outer = is_outer(me, count)
    kept, sent = choose(me, size, shifts[0])
    for comp in range(2):
        for lane in range(0, first.shape[2], LANES):
            here = slice(lane, lane + LANES)
            one = first[comp, :, here]
            two = jnp.where(outer, slot_a[comp, :, here], slot_b[comp, :, here])
            keep[comp, :, here] = jnp.where(kept, one, two)
            send[comp, :, here] = jnp.where(sent, one, two)


def pair_kernel(count, place, keep, slot_a, slot_b, pair):
    outer = is_outer(place[1], count)
    pair[0:2] = keep[...]

    @pl.when(outer)
    def _():
        pair[2:4] = slot_a[:, :, : pair.shape[2]]

    @pl.when(jnp.logical_not(outer))
    def _():
        pair[2:4] = slot_b[:, :, : pair.shape[2]]


def flux_kernel(parts, row0, place, table, plan, iron, weights, pair, far, *refs):
    *outs, flux, result = refs
    total = outs[0].shape[2]
    tm, me = place[0], place[1]
    source = [((me + plan[1 + m] - plan[0]) ^ me) & 3 for m in range(2)]
    is_near = [s == 0 for s in source]
    is_two = [s == 2 for s in source]
    is_one = [s == 1 for s in source]
    quarter = tm * (iron.shape[0] // parts) + row0
    for lane in range(0, total, LANES):
        here = slice(lane, lane + LANES)
        there = slice(row0 * LANES + lane, row0 * LANES + lane + LANES)
        field = []
        for comp in range(2):
            blocks = [ref[c, :, here] for ref in (pair, far) for c in (comp, 2 + comp)]
            terms = [
                weights[m, :, there]
                * jnp.where(
                    is_near[m],
                    blocks[0],
                    jnp.where(is_two[m], blocks[1], jnp.where(is_one[m], blocks[2], blocks[3])),
                )
                for m in range(2)
            ]
            field.append(terms[0] + terms[1])
        square = field[0] * field[0] + field[1] * field[1]
        gain = iron[pl.ds(quarter + lane // LANES, 1), :] * (1.0 + square / (1.0 + square))
        for comp in range(2):
            flux[:, comp * total + lane : comp * total + lane + LANES] = gain * field[comp]
    result[...] = table_dot(table[...], flux[...])
    rows = result.shape[0] // parts
    for i in range(parts):
        first = pl.multiple_of((tm ^ i) * rows, rows)
        for comp in range(2):
            outs[i][comp] = result[pl.ds(first, rows), comp * total : (comp + 1) * total]


def finish_kernel(parts, chunks, place, source, *refs):
    pieces, (out, made, sems) = refs[:-3], refs[-3:]
    share_rows = source.shape[2] // parts
    copies = []
    for i in range(parts):
        first = pl.multiple_of((place[0] ^ i) * share_rows, SUBLANES)
        for comp in range(2):
            rows = [
                pieces[g * parts + i][comp, :, lane : lane + LANES]
                for g in range(chunks)
                for lane in range(0, pieces[g * parts].shape[2], LANES)
            ]
            for row in range(0, share_rows, SUBLANES):
                turned = jnp.swapaxes(jnp.stack(rows[row : row + SUBLANES]), 0, 1)
                made[i, :, comp, row : row + SUBLANES, :] = turned - source[:, comp, pl.ds(first + row, SUBLANES), :]
        copies.append(
            pltpu.make_async_copy(made.at[i], out.at[:, :, pl.ds(first, share_rows), :], sems.at[i])
        )
        copies[i].start()
    for copy in copies:
        copy.wait()


def body(rotor_coeffs, mortar_weights, block_shifts, stencil_offsets, reluctivity, source):
    parts, count = lax.axis_size("tm"), lax.axis_size("azim")
    coeff_rows, comps, _, nodes = rotor_coeffs.shape
    sample_rows = mortar_weights.shape[0]
    coeffs, samples = coeff_rows * parts, sample_rows * parts
    share_rows = nodes // parts // LANES
    bounds = np.cumsum((0,) + CHUNK_SHARES) * share_rows // sum(CHUNK_SHARES)
    heights = [int(h) for h in np.diff(bounds)]
    widths = [h * LANES for h in heights]
    chunks = len(heights)
    place = jnp.stack([lax.axis_index("tm"), lax.axis_index("azim")]).astype(jnp.int32)
    table = basis_table(samples, coeffs)
    forward = jnp.asarray(split_table(table))
    backward = jnp.asarray(split_table(np.ascontiguousarray(table.T) * np.float32(2.0 / samples)))
    gates = {}

    def in_rows(x):
        return x.reshape(x.shape[0], comps, nodes // LANES, LANES)

    def pack(x, spans, after=(), plan=(), limit=LIMIT):
        low = spans[0][0] // SUBLANES * SUBLANES
        high = -(-(spans[-1][0] + spans[-1][1]) // SUBLANES) * SUBLANES
        shape = (2, x.shape[0], (spans[0][1] + bool(plan)) * LANES)
        *outs, token = call(
            functools.partial(plan_pack_kernel if plan else pack_kernel, parts, spans),
            [f32(*shape)] * parts,
            (place, in_rows(x), *plan),
            after=after,
            scratch=(
                pltpu.VMEM((parts, x.shape[0], comps, high - low, LANES), jnp.float32),
                pltpu.SemaphoreType.DMA((parts,)),
            ),
            smem=(0, 2, 3) if plan else (0,),
            hbm=(1,),
            limit=limit,
        )
        return outs, token

    def swap(pieces):
        return [pieces[0]] + [xor_permute(pieces[i], "tm", i) for i in range(1, parts)]

    def gather(pieces, lanes, rows, after=()):
        *outs, token = call(
            functools.partial(gather_kernel, parts),
            [f32(2, rows, w) for w in lanes],
            (place, *pieces),
            after=after,
        )
        return outs, token

    head, token = pack(rotor_coeffs, [(0, heights[0])], limit=FULL)
    rest, token = pack(
        rotor_coeffs,
        [(heights[0], share_rows - heights[0])],
        after=(token,),
        plan=(block_shifts, stencil_offsets.T),
    )
    (own_first,), token = gather(swap(head), widths[:1], coeffs, (token,))
    *own_rest, plan, token = call(
        functools.partial(plan_gather_kernel, parts),
        [f32(2, coeffs, w) for w in widths[1:]] + [jax.ShapeDtypeStruct((3, samples, LANES), jnp.int32)],
        (place, *swap(rest)),
        after=(token,),
    )
    own = [own_first] + own_rest
    weights, token = pack(mortar_weights, [(0, share_rows)], after=(token,))
    gates[1] = [token]
    (weights,), token = gather(swap(weights), [share_rows * LANES], samples)
    gates[3] = [token]

    half, fourth = count // 2, count // 4
    outer = [d for d in range(count) if is_outer(d, count)]
    inner = [d for d in range(count) if not is_outer(d, count)]
    coeff_a = [(d, d ^ half) for d in outer]
    coeff_b = [(d, d ^ half) for d in inner]
    sample_a = [(d, d ^ fourth) for d in inner]
    sample_b = [(d, d ^ fourth) for d in outer]

    def neighbours(keep, slot_a, slot_b, after):
        size = count // 8
        while size >= 2:
            send, keep, _ = call(
                functools.partial(middle_kernel, count, size), [keep, keep], (place, plan, keep, slot_a, slot_b)
            )
            slot_a = slot_b = xor_permute(send, "azim", size)
            size //= 2
        pair, token = call(
            functools.partial(pair_kernel, count),
            [f32(4, samples, keep.shape[2])],
            (place, keep, slot_a, slot_b),
            after=after,
        )
        return pair, xor_permute(pair, "azim", 1), token

    iron = reluctivity.reshape(nodes // LANES, LANES)

    def flux(k, pair, far):
        total = widths[k]
        *made, token = call(
            functools.partial(flux_kernel, parts, sum(heights[:k])),
            [f32(2, coeff_rows, total)] * parts,
            (place, backward, plan, iron, weights, pair, far),
            scratch=(pltpu.VMEM((samples, 2 * total), jnp.float32), pltpu.VMEM((coeffs, 2 * total), jnp.float32)),
            flops=4 * samples * 3 * coeffs * total,
        )
        return swap(made), token

    slots_a, slots_b, keeps, pieces = [], [], [], []
    send_a = send_b = own[0]
    for k in range(chunks):
        slots_a.append(lax.ppermute(send_a, "azim", coeff_a + (sample_a if k else [])))
        slots_b.append(lax.ppermute(send_b, "azim", coeff_b + (sample_b if k else [])))
        after = own[k + 1] if k + 1 < chunks else own[k]
        block, sent = f32(2, samples, widths[k]), f32(2, samples, max(widths[k], after.shape[2]))
        flops = 8 * samples * 3 * coeffs * widths[k]
        send_a, kept, _ = call(
            functools.partial(first_kernel, count),
            [sent, block],
            (place, forward, plan, own[k], slots_a[k], after),
            after=gates.get(k, ()),
            flops=flops,
        )
        send_b, kept, token = call(
            functools.partial(second_kernel, count),
            [sent, block],
            (place, forward, plan, own[k], slots_b[k], after, kept),
            flops=flops,
        )
        keeps.append(kept)
        if k:
            *pair, token = neighbours(keeps[k - 1], slots_a[k], slots_b[k], (token,))
            gates.setdefault(k + 1, []).append(token)
            made, token = flux(k - 1, *pair)
            pieces += made
            gate = gates.setdefault(min(k - 1 + FLUX_GATE, chunks), [])
            gate.append(token)
            if k - 1 in SEEN:
                gate += call(functools.partial(seen_kernel), [], (place, *made))
    slot_a = lax.ppermute(send_a, "azim", sample_a)
    slot_b = lax.ppermute(send_b, "azim", sample_b)
    *pair, _ = neighbours(keeps[-1], slot_a, slot_b, gates.get(chunks, ()))
    pieces += flux(chunks - 1, *pair)[0]
    out, _ = call(
        functools.partial(finish_kernel, parts, chunks),
        [f32(coeff_rows, comps, nodes // LANES, LANES)],
        (place, in_rows(source), *pieces),
        scratch=(
            pltpu.VMEM((parts, coeff_rows, comps, share_rows, LANES), jnp.float32),
            pltpu.SemaphoreType.DMA((parts,)),
        ),
        out_hbm=True,
    )
    return out.reshape(source.shape)


def solution(mesh):
    wide = P("tm", None, "azim", None)
    in_specs = (wide, wide, P("tm"), P("tm", None), P("azim", None), wide)
    return jax.shard_map(body, mesh=mesh, in_specs=in_specs, out_specs=wide, check_vma=False)
```

```python
import functools

import jax
import jax.numpy as jnp
import ml_dtypes
import numpy as np
from jax import lax
from jax.experimental import pallas as pl
from jax.experimental.pallas import tpu as pltpu
from jax.sharding import PartitionSpec as P

LANES = 128
CHUNK_SHARES = (8, 8, 8, 8)
FLUX_GATE = 3
SEEN = (0, 1)
VMEM = pl.BlockSpec(memory_space=pltpu.VMEM)
SMEM = pl.BlockSpec(memory_space=pltpu.SMEM)
HBM = pl.BlockSpec(memory_space=pltpu.HBM)
SUBLANES = 8
LIMIT = 48 * 1024 * 1024
FULL = 62 * 1024 * 1024


def basis_table(sample_count, coefficient_count):
    column = np.arange(coefficient_count)
    order = 2 * (column // 2) + 1
    phase = order[None, :] * (2 * np.arange(sample_count)[:, None] + 1) % (4 * sample_count)
    angle = phase * (np.pi / (2 * sample_count))
    return np.where(column[None, :] % 2 == 0, np.cos(angle), np.sin(angle)).astype(np.float32)


def split_table(table):
    high = table.astype(ml_dtypes.bfloat16)
    low = (table - high.astype(np.float32)).astype(ml_dtypes.bfloat16)
    return np.concatenate([high, high, low], axis=1)


def table_dot(parts, value):
    high = value.astype(jnp.bfloat16)
    low = (value - high.astype(jnp.float32)).astype(jnp.bfloat16)
    return jnp.dot(
        parts, jnp.concatenate([high, low, high], axis=0), preferred_element_type=jnp.float32
    )


def f32(*shape):
    return jax.ShapeDtypeStruct(shape, jnp.float32)


TOKEN = f32(SUBLANES, LANES)


def call(kernel, out_shape, inputs, after=(), scratch=(), flops=0, smem=(0,), hbm=(), out_hbm=False, limit=LIMIT):
    count, tokens, made = len(inputs), len(after), len(out_shape)
    size = sum(4 * np.prod(x.shape) for x in (*inputs, *out_shape))

    def run(*refs):
        outs = refs[count + tokens : count + tokens + made]
        token, rest = refs[count + tokens + made], refs[count + tokens + made + 1 :]
        token[...] = jnp.zeros_like(token)
        kernel(*refs[:count], *outs, *rest)

    return pl.pallas_call(
        run,
        name=kernel.func.__name__,
        out_shape=[jax.ShapeDtypeStruct(x.shape, x.dtype) for x in (*out_shape, TOKEN)],
        in_specs=[SMEM if n in smem else HBM if n in hbm else VMEM for n in range(count)] + [VMEM] * tokens,
        out_specs=[HBM if out_hbm else VMEM] * made + [VMEM],
        scratch_shapes=list(scratch),
        compiler_params=pltpu.CompilerParams(vmem_limit_bytes=limit),
        cost_estimate=pl.CostEstimate(flops=flops, bytes_accessed=int(size), transcendentals=0),
    )(*inputs, *after)


def xor_permute(value, axis, step):
    count = lax.axis_size(axis)
    return lax.ppermute(value, axis, [(i, i ^ step) for i in range(count)])


def store_rows(block, row, spans, outs):
    turned = jnp.swapaxes(block, 0, 1)
    for r in range(SUBLANES):
        for (first, length), out in zip(spans, outs):
            if first <= row + r < first + length:
                lane = (row + r - first) * LANES
                out[:, lane : lane + LANES] = turned[r]


def pack_kernel(parts, spans, place, x, *refs):
    outs, (staged, sems) = refs[:-2], refs[-2:]
    share_rows = x.shape[2] // parts
    low = spans[0][0] // SUBLANES * SUBLANES
    copies = []
    for i in range(parts):
        first = pl.multiple_of((place[0] ^ i) * share_rows + low, SUBLANES)
        copies.append(
            pltpu.make_async_copy(x.at[:, :, pl.ds(first, staged.shape[3]), :], staged.at[i], sems.at[i])
        )
        copies[i].start()
    for i in range(parts):
        copies[i].wait()
        for comp in range(2):
            for row in range(0, staged.shape[3], SUBLANES):
                store_rows(
                    staged[i, :, comp, row : row + SUBLANES, :],
                    low + row,
                    spans,
                    [out.at[comp] for out in outs[i * len(spans) : (i + 1) * len(spans)]],
                )


def plan_pack_kernel(parts, spans, place, x, shifts, offsets, *refs):
    outs = refs[: parts * len(spans)]
    pack_kernel(parts, spans, place, x, *refs)
    rows = shifts.shape[0]
    row = lax.broadcasted_iota(jnp.int32, (rows, LANES), 0)
    lane = lax.broadcasted_iota(jnp.int32, (rows, LANES), 1)
    plan = jnp.zeros((rows, LANES), jnp.int32)
    for j in range(rows):
        numbers = jnp.where(lane == 0, shifts[j], jnp.where(lane == 1, offsets[0, j], offsets[1, j]))
        plan = jnp.where(row == j, numbers, plan)
    for i in range(parts):
        out = outs[i * len(spans)]
        behind = spans[0][1] * LANES
        out[0, :, behind:] = plan.astype(jnp.float32)
        out[1, :, behind:] = jnp.zeros(plan.shape, jnp.float32)


def seen_kernel(place, *pieces):
    pass


def gather_kernel(parts, place, *refs):
    pieces, outs = refs[:parts], refs[parts:]
    rows = pieces[0].shape[1]
    for i in range(parts):
        first = pl.multiple_of((place[0] ^ i) * rows, rows)
        lane = 0
        for out in outs:
            out[:, pl.ds(first, rows), :] = pieces[i][:, :, lane : lane + out.shape[2]]
            lane += out.shape[2]


def plan_gather_kernel(parts, place, *refs):
    pieces, (*outs, plan) = refs[:parts], refs[parts:]
    gather_kernel(parts, place, *pieces, *outs)
    rows = pieces[0].shape[1]
    behind = sum(out.shape[2] for out in outs)
    for i in range(parts):
        first = pl.multiple_of((place[0] ^ i) * rows, rows)
        numbers = pieces[i][0, :, behind:].astype(jnp.int32)
        for n in range(3):
            plan[n, pl.ds(first, rows), :] = jnp.broadcast_to(numbers[:, n : n + 1], (rows, LANES))


def in_first(me, base, size, shifts):
    offset = (me - base + 1 + shifts) & (2 * size - 1)
    return ((base - 1 - shifts + offset - me) & (4 * size - 1)) == 0


def choose(me, size, shifts):
    clear = ~(size - 1)
    kept = in_first(me, me & clear, size, shifts)
    sent = in_first(me, (me ^ size) & clear, size, shifts)
    return kept, sent


def is_outer(me, count):
    return ((me // (count // 2)) ^ (me // (count // 4))) & 1 == 0


def sample_step(count, place, table, shifts, own, far, send, keep):
    me = place[1]
    kept, sent = choose(me, count // 4, shifts[0])
    parts = table[...]
    for comp in range(2):
        near_samples = table_dot(parts, own[comp])
        far_samples = table_dot(parts, far[comp, :, : own.shape[2]])
        for lane in range(0, own.shape[2], LANES):
            here = slice(lane, lane + LANES)
            keep[comp, :, here] = jnp.where(kept, near_samples[:, here], far_samples[:, here])
            send[comp, :, here] = jnp.where(sent, near_samples[:, here], far_samples[:, here])


def copy_lanes(source, target):
    width = min(source.shape[2], target.shape[2])
    target[:, :, :width] = source[:, :, :width]


def first_kernel(count, place, table, shifts, own, arrived, following, send, keep):
    outer = is_outer(place[1], count)

    @pl.when(outer)
    def _():
        copy_lanes(following, send)
        keep[...] = own[...]

    @pl.when(jnp.logical_not(outer))
    def _():
        sample_step(count, place, table, shifts, own, arrived, send, keep)


def second_kernel(count, place, table, shifts, own, arrived, following, kept, send, keep):
    outer = is_outer(place[1], count)

    @pl.when(outer)
    def _():
        sample_step(count, place, table, shifts, own, arrived, send, keep)

    @pl.when(jnp.logical_not(outer))
    def _():
        copy_lanes(following, send)
        keep[...] = kept[...]


def middle_kernel(count, size, place, shifts, first, slot_a, slot_b, send, keep):
    me = place[1]
    outer = is_outer(me, count)
    kept, sent = choose(me, size, shifts[0])
    for comp in range(2):
        for lane in range(0, first.shape[2], LANES):
            here = slice(lane, lane + LANES)
            one = first[comp, :, here]
            two = jnp.where(outer, slot_a[comp, :, here], slot_b[comp, :, here])
            keep[comp, :, here] = jnp.where(kept, one, two)
            send[comp, :, here] = jnp.where(sent, one, two)


def pair_kernel(count, place, keep, slot_a, slot_b, pair):
    outer = is_outer(place[1], count)
    pair[0:2] = keep[...]

    @pl.when(outer)
    def _():
        pair[2:4] = slot_a[:, :, : pair.shape[2]]

    @pl.when(jnp.logical_not(outer))
    def _():
        pair[2:4] = slot_b[:, :, : pair.shape[2]]


def flux_kernel(parts, row0, place, table, plan, iron, weights, pair, far, *refs):
    *outs, flux, result = refs
    total = outs[0].shape[2]
    tm, me = place[0], place[1]
    source = [((me + plan[1 + m] - plan[0]) ^ me) & 3 for m in range(2)]
    is_near = [s == 0 for s in source]
    is_two = [s == 2 for s in source]
    is_one = [s == 1 for s in source]
    quarter = tm * (iron.shape[0] // parts) + row0
    for lane in range(0, total, LANES):
        here = slice(lane, lane + LANES)
        there = slice(row0 * LANES + lane, row0 * LANES + lane + LANES)
        field = []
        for comp in range(2):
            blocks = [ref[c, :, here] for ref in (pair, far) for c in (comp, 2 + comp)]
            terms = [
                weights[m, :, there]
                * jnp.where(
                    is_near[m],
                    blocks[0],
                    jnp.where(is_two[m], blocks[1], jnp.where(is_one[m], blocks[2], blocks[3])),
                )
                for m in range(2)
            ]
            field.append(terms[0] + terms[1])
        square = field[0] * field[0] + field[1] * field[1]
        gain = iron[pl.ds(quarter + lane // LANES, 1), :] * (1.0 + square / (1.0 + square))
        for comp in range(2):
            flux[:, comp * total + lane : comp * total + lane + LANES] = gain * field[comp]
    result[...] = table_dot(table[...], flux[...])
    rows = result.shape[0] // parts
    for i in range(parts):
        first = pl.multiple_of((tm ^ i) * rows, rows)
        for comp in range(2):
            outs[i][comp] = result[pl.ds(first, rows), comp * total : (comp + 1) * total]


def less_source(parts, chunks, row0, height, place, source, pieces, made):
    share_rows = source.shape[2] // parts
    for i in range(parts):
        first = pl.multiple_of((place[0] ^ i) * share_rows, SUBLANES) + row0
        for comp in range(2):
            rows = [
                pieces[g * parts + i][comp, :, lane : lane + LANES]
                for g in range(chunks)
                for lane in range(0, pieces[g * parts].shape[2], LANES)
            ]
            for row in range(0, height, SUBLANES):
                turned = jnp.swapaxes(jnp.stack(rows[row : row + SUBLANES]), 0, 1)
                here = pl.ds(pl.multiple_of(first + row, SUBLANES), SUBLANES)
                made[i, :, comp, row : row + SUBLANES, :] = turned - source[:, comp, here, :]


def early_kernel(parts, chunks, place, source, *refs):
    less_source(parts, chunks, 0, refs[-1].shape[3], place, source, refs[:-1], refs[-1])


def finish_kernel(parts, chunks, place, source, early, *refs):
    pieces, (out, made, sems) = refs[:-3], refs[-3:]
    share_rows = source.shape[2] // parts
    early_rows, late_rows = early.shape[3], made.shape[3]
    copies = []
    for i in range(parts):
        first = pl.multiple_of((place[0] ^ i) * share_rows, SUBLANES)
        here = pl.ds(first, early_rows)
        there = pl.ds(pl.multiple_of(first + early_rows, SUBLANES), late_rows)
        copies.append(pltpu.make_async_copy(early.at[i], out.at[:, :, here, :], sems.at[0, i]))
        copies.append(pltpu.make_async_copy(made.at[i], out.at[:, :, there, :], sems.at[1, i]))
        copies[2 * i].start()
    less_source(parts, chunks, early_rows, late_rows, place, source, pieces, made)
    for i in range(parts):
        copies[2 * i + 1].start()
    for copy in copies:
        copy.wait()


def body(rotor_coeffs, mortar_weights, block_shifts, stencil_offsets, reluctivity, source):
    parts, count = lax.axis_size("tm"), lax.axis_size("azim")
    coeff_rows, comps, _, nodes = rotor_coeffs.shape
    sample_rows = mortar_weights.shape[0]
    coeffs, samples = coeff_rows * parts, sample_rows * parts
    share_rows = nodes // parts // LANES
    bounds = np.cumsum((0,) + CHUNK_SHARES) * share_rows // sum(CHUNK_SHARES)
    heights = [int(h) for h in np.diff(bounds)]
    widths = [h * LANES for h in heights]
    chunks = len(heights)
    place = jnp.stack([lax.axis_index("tm"), lax.axis_index("azim")]).astype(jnp.int32)
    table = basis_table(samples, coeffs)
    forward = jnp.asarray(split_table(table))
    backward = jnp.asarray(split_table(np.ascontiguousarray(table.T) * np.float32(2.0 / samples)))
    gates = {}

    def in_rows(x):
        return x.reshape(x.shape[0], comps, nodes // LANES, LANES)

    def pack(x, spans, after=(), plan=(), limit=LIMIT):
        low = spans[0][0] // SUBLANES * SUBLANES
        high = -(-(spans[-1][0] + spans[-1][1]) // SUBLANES) * SUBLANES
        shape = (2, x.shape[0], (spans[0][1] + bool(plan)) * LANES)
        *outs, token = call(
            functools.partial(plan_pack_kernel if plan else pack_kernel, parts, spans),
            [f32(*shape)] * parts,
            (place, in_rows(x), *plan),
            after=after,
            scratch=(
                pltpu.VMEM((parts, x.shape[0], comps, high - low, LANES), jnp.float32),
                pltpu.SemaphoreType.DMA((parts,)),
            ),
            smem=(0, 2, 3) if plan else (0,),
            hbm=(1,),
            limit=limit,
        )
        return outs, token

    def swap(pieces):
        return [pieces[0]] + [xor_permute(pieces[i], "tm", i) for i in range(1, parts)]

    def gather(pieces, lanes, rows, after=()):
        *outs, token = call(
            functools.partial(gather_kernel, parts),
            [f32(2, rows, w) for w in lanes],
            (place, *pieces),
            after=after,
        )
        return outs, token

    head, token = pack(rotor_coeffs, [(0, heights[0])], limit=FULL)
    rest, token = pack(
        rotor_coeffs,
        [(heights[0], share_rows - heights[0])],
        after=(token,),
        plan=(block_shifts, stencil_offsets.T),
    )
    (own_first,), token = gather(swap(head), widths[:1], coeffs, (token,))
    *own_rest, plan, token = call(
        functools.partial(plan_gather_kernel, parts),
        [f32(2, coeffs, w) for w in widths[1:]] + [jax.ShapeDtypeStruct((3, samples, LANES), jnp.int32)],
        (place, *swap(rest)),
        after=(token,),
    )
    own = [own_first] + own_rest
    weights, token = pack(mortar_weights, [(0, share_rows)], after=(token,))
    gates[1] = [token]
    (weights,), token = gather(swap(weights), [share_rows * LANES], samples)
    gates[3] = [token]

    half, fourth = count // 2, count // 4
    outer = [d for d in range(count) if is_outer(d, count)]
    inner = [d for d in range(count) if not is_outer(d, count)]
    coeff_a = [(d, d ^ half) for d in outer]
    coeff_b = [(d, d ^ half) for d in inner]
    sample_a = [(d, d ^ fourth) for d in inner]
    sample_b = [(d, d ^ fourth) for d in outer]

    def neighbours(keep, slot_a, slot_b, after):
        size = count // 8
        while size >= 2:
            send, keep, _ = call(
                functools.partial(middle_kernel, count, size), [keep, keep], (place, plan, keep, slot_a, slot_b)
            )
            slot_a = slot_b = xor_permute(send, "azim", size)
            size //= 2
        pair, token = call(
            functools.partial(pair_kernel, count),
            [f32(4, samples, keep.shape[2])],
            (place, keep, slot_a, slot_b),
            after=after,
        )
        return pair, xor_permute(pair, "azim", 1), token

    iron = reluctivity.reshape(nodes // LANES, LANES)

    def flux(k, pair, far):
        total = widths[k]
        *made, token = call(
            functools.partial(flux_kernel, parts, sum(heights[:k])),
            [f32(2, coeff_rows, total)] * parts,
            (place, backward, plan, iron, weights, pair, far),
            scratch=(pltpu.VMEM((samples, 2 * total), jnp.float32), pltpu.VMEM((coeffs, 2 * total), jnp.float32)),
            flops=4 * samples * 3 * coeffs * total,
        )
        return swap(made), token

    slots_a, slots_b, keeps, pieces = [], [], [], []
    send_a = send_b = own[0]
    for k in range(chunks):
        slots_a.append(lax.ppermute(send_a, "azim", coeff_a + (sample_a if k else [])))
        slots_b.append(lax.ppermute(send_b, "azim", coeff_b + (sample_b if k else [])))
        after = own[k + 1] if k + 1 < chunks else own[k]
        block, sent = f32(2, samples, widths[k]), f32(2, samples, max(widths[k], after.shape[2]))
        flops = 8 * samples * 3 * coeffs * widths[k]
        send_a, kept, _ = call(
            functools.partial(first_kernel, count),
            [sent, block],
            (place, forward, plan, own[k], slots_a[k], after),
            after=gates.get(k, ()),
            flops=flops,
        )
        send_b, kept, token = call(
            functools.partial(second_kernel, count),
            [sent, block],
            (place, forward, plan, own[k], slots_b[k], after, kept),
            flops=flops,
        )
        keeps.append(kept)
        if k:
            *pair, token = neighbours(keeps[k - 1], slots_a[k], slots_b[k], (token,))
            gates.setdefault(k + 1, []).append(token)
            made, token = flux(k - 1, *pair)
            pieces += made
            gate = gates.setdefault(min(k - 1 + FLUX_GATE, chunks), [])
            gate.append(token)
            if k - 1 == SEEN[-1]:
                early_rows = sum(heights[:k])
                early, token = call(
                    functools.partial(early_kernel, parts, k),
                    [f32(parts, coeff_rows, comps, early_rows, LANES)],
                    (place, in_rows(source), *pieces),
                )
                gate.append(token)
            elif k - 1 in SEEN:
                gate += call(functools.partial(seen_kernel), [], (place, *made))
    slot_a = lax.ppermute(send_a, "azim", sample_a)
    slot_b = lax.ppermute(send_b, "azim", sample_b)
    *pair, _ = neighbours(keeps[-1], slot_a, slot_b, gates.get(chunks, ()))
    pieces += flux(chunks - 1, *pair)[0]
    out, _ = call(
        functools.partial(finish_kernel, parts, chunks - len(SEEN)),
        [f32(coeff_rows, comps, nodes // LANES, LANES)],
        (place, in_rows(source), early, *pieces[len(SEEN) * parts :]),
        scratch=(
            pltpu.VMEM((parts, coeff_rows, comps, share_rows - early_rows, LANES), jnp.float32),
            pltpu.SemaphoreType.DMA((2, parts)),
        ),
        out_hbm=True,
    )
    return out.reshape(source.shape)


def solution(mesh):
    wide = P("tm", None, "azim", None)
    in_specs = (wide, wide, P("tm"), P("tm", None), P("azim", None), wide)
    return jax.shard_map(body, mesh=mesh, in_specs=in_specs, out_specs=wide, check_vma=False)
```
